512 devices in a mesh: dp: 32 (over y_lo, z), tensor: 16 (over y_hi, x, core).
Axes of the slice: x: 4, y: 4 (y_hi: 2, y_lo: 2; y = y_hi * 2 + y_lo), z: 16, core: 2. Of those that a mesh axis runs over, the one named last changes fastest.
Arguments:
- tokens: bfloat16 [12288, 3072], P(('dp', 'tensor')), may hold values from -6 to 6
- cotangent: bfloat16 [12288, 3072], P(('dp', 'tensor')), may hold values from -0.119628906 to 0.119628906
- up_blocks: bfloat16 [320, 256, 256], P('tensor', 'dp'), may hold values from -0.15625 to 0.15625
- down_blocks: bfloat16 [320, 256, 256], P('tensor', 'dp'), may hold values from -0.078125 to 0.078125
- up_index: int32 [320], P('tensor'), may hold values from 0 to 35, as said below
- up_count: int32 [16], P('tensor'), may hold values from 10 to 20, as said below
- down_index: int32 [320], P('tensor'), may hold values from 0 to 35, as said below
- down_count: int32 [16], P('tensor'), may hold values from 10 to 20, as said below
Outputs:
- mixed: bfloat16 [12288, 3072], P(('dp', 'tensor'))
- up_grad: float32 [320, 256, 256], P('tensor', 'dp')
- down_grad: float32 [320, 256, 256], P('tensor', 'dp')
The draws below stay inside these ranges and needn't reach their ends.
Inputs may be any that keep to these rules, and one draw needn't show every extreme that they name: `up_index`: the 20 numbers of one tensor shard are distinct. `up_count`: some shard holds exactly 20, another exactly the least. `down_index`: the 20 numbers of one tensor shard are distinct. `down_count`: some shard holds exactly 20, another exactly the least.
All inputs are finite; a program needn't handle non-finite values.
Results may differ from the reference program's by a relative error of at most 0.018.
Values may be sent and summed in bfloat16 or wider, within the bound.
No kernel may reach another device: no remote copies, remote signals or barrier semaphores. Data moves between devices by JAX's collectives and lax.ppermute only.
A program may use at most 64 MiB of HBM per device.

```python
import jax
import jax.numpy as jnp
from jax import lax

D = 3072
FF = 12288
BLK = 256
TOK_DEV = 384
TOKENS = 12288
DB = 12
HBL = 3
NBS = 36
CAP = 20
SLOTS = 320
N_DP = 32
N_TENSOR = 16


def kept_blocks(key, salt):
    key = jax.random.fold_in(key, salt)
    count_key, pick_key, order_key = jax.random.split(key, 3)
    lowest = max(1, CAP // 2)
    counts = jax.random.randint(count_key, (N_TENSOR,), lowest, CAP + 1)
    fullest = jax.random.randint(pick_key, (), 0, N_TENSOR)
    emptiest = (fullest + 1) % N_TENSOR
    shard_ids = jnp.arange(N_TENSOR)
    counts = jnp.where(shard_ids == fullest, CAP, counts)
    counts = jnp.where(shard_ids == emptiest, lowest, counts)
    order_keys = jax.random.split(order_key, N_TENSOR)

    def shard_order(single):
        return jax.random.permutation(single, NBS)[:CAP]
    orders = jax.vmap(shard_order)(order_keys)
    return (orders.reshape(SLOTS).astype(jnp.int32), counts.astype(jnp.int32))


def draw_up_index(key, part):
    return kept_blocks(key, 11)[0]


def draw_up_count(key, part):
    return kept_blocks(key, 11)[1]


def draw_down_index(key, part):
    return kept_blocks(key, 23)[0]


def draw_down_count(key, part):
    return kept_blocks(key, 23)[1]


def steps_of(own_key, dims, cuts, low, high):
    def one(axis_at, shards_of):
        draws = jax.random.uniform(jax.random.fold_in(jax.random.fold_in(own_key, 6), axis_at), (shards_of,), jnp.float32, low / len(cuts), high / len(cuts))
        return jnp.repeat(jnp.exp(draws), dims[axis_at] // shards_of).reshape((-1,) + (1,) * (len(dims) - axis_at - 1))

    gain = one(*cuts[0])
    for cut in cuts[1:]:
        gain = gain * one(*cut)
    return gain


def normal_values(own_key, shape, width, reach, cuts=(), kind=jnp.bfloat16):
    array = width * jax.random.normal(own_key, shape, jnp.float32)
    if cuts:
        array = array * steps_of(own_key, shape, cuts, -0.22, 0.18)
    return jnp.clip(array, -reach, reach).astype(kind)


def setup_inputs(seed: int = 0) -> dict:
    keys = jax.random.split(jax.random.key(seed), 9)
    return {
        "tokens": normal_values(keys[0], (TOKENS, D), 1.0, 6.0, ((0, 512),)),
        "cotangent": normal_values(keys[1], (TOKENS, D), 0.02, 0.119628906, ((0, 512),)),
        "up_blocks": normal_values(keys[2], (SLOTS, BLK, BLK), (D * CAP // NBS) ** -0.5, 0.15625, ((0, 16), (1, 32))),
        "down_blocks": normal_values(keys[3], (SLOTS, BLK, BLK), (FF * CAP // NBS) ** -0.5, 0.078125, ((0, 16), (1, 32))),
        "up_index": draw_up_index(jax.random.fold_in(keys[8], 71), 0),
        "up_count": draw_up_count(jax.random.fold_in(keys[8], 71), 0),
        "down_index": draw_down_index(jax.random.fold_in(keys[8], 71), 0),
        "down_count": draw_down_count(jax.random.fold_in(keys[8], 71), 0),
    }


GELU_C = 0.7978845608028654


def gelu_value(value):
    return 0.5 * value * (1.0 + jnp.tanh(GELU_C * (value + 0.044715 * value * value * value)))


def gelu_slope(value):
    bent = jnp.tanh(GELU_C * (value + 0.044715 * value * value * value))
    return 0.5 * (1.0 + bent) + 0.5 * value * (1.0 - bent * bent) * GELU_C * (1.0 + 3.0 * 0.044715 * value * value)


def slot_layout(index, count, per_row):
    row_block = (index // per_row).astype(jnp.int32)
    column_block = (index % per_row).astype(jnp.int32)
    live = (jnp.arange(index.shape[0], dtype=jnp.int32) < count).astype(jnp.float32)
    return row_block, column_block, live


def one_hot(labels, number, live):
    return (labels[:, None] == jnp.arange(number, dtype=jnp.int32)[None, :]).astype(jnp.float32) * live[:, None]


def group_sum(left, right, live):
    left = left.reshape(N_DP, TOK_DEV, CAP, BLK)
    right = right.reshape(N_DP, TOK_DEV, CAP, BLK)
    terms = jnp.einsum("gtsk,gtsn->gskn", left, right, precision=lax.Precision.HIGHEST)
    terms = (terms * live[None, :, None, None]).astype(jnp.bfloat16)
    terms = lax.optimization_barrier(terms).astype(jnp.float32)
    return jnp.sum(terms, axis=0)


def reference(tokens, cotangent, up_blocks, down_blocks, up_index, up_count, down_index, down_count):
    highest = lax.Precision.HIGHEST
    x_blocks = tokens.reshape(TOKENS, DB, BLK)
    dy_blocks = cotangent.reshape(TOKENS, DB, BLK)
    pieces = (up_blocks.reshape(N_TENSOR, CAP, BLK, BLK), down_blocks.reshape(N_TENSOR, CAP, BLK, BLK),
              up_index.reshape(N_TENSOR, CAP), up_count, down_index.reshape(N_TENSOR, CAP), down_count)

    def one_shard(total, piece):
        up_w, down_w, up_idx, up_cnt, down_idx, down_cnt = piece
        up_row, up_col, up_live = slot_layout(up_idx, up_cnt, HBL)
        down_row, down_col, down_live = slot_layout(down_idx, down_cnt, HBL)
        up_w = up_w.astype(jnp.float32)
        down_w = down_w.astype(jnp.float32)
        x_slots = jnp.take(x_blocks, up_row, axis=1).astype(jnp.float32)
        pre_slots = jnp.einsum("tsk,skn->stn", x_slots, up_w, precision=highest)
        pre = jnp.einsum("stn,sh->thn", pre_slots, one_hot(up_col, HBL, up_live), precision=highest)
        hidden = gelu_value(pre).astype(jnp.bfloat16)
        h_slots = jnp.take(hidden, down_col, axis=1).astype(jnp.float32)
        out_slots = jnp.einsum("tsk,skn->stn", h_slots, down_w, precision=highest)
        partial_value = jnp.einsum("stn,sd->tdn", out_slots, one_hot(down_row, DB, down_live), precision=highest)
        partial_value = partial_value.reshape(TOKENS, D).astype(jnp.bfloat16)
        partial_value = lax.optimization_barrier(partial_value).astype(jnp.float32)
        dy_slots = jnp.take(dy_blocks, down_row, axis=1).astype(jnp.float32)
        down_terms = group_sum(h_slots, dy_slots, down_live)
        back_slots = jnp.einsum("tsn,skn->stk", dy_slots, down_w, precision=highest)
        back = jnp.einsum("stk,sh->thk", back_slots, one_hot(down_col, HBL, down_live), precision=highest)
        pre_grad = (back * gelu_slope(pre)).astype(jnp.bfloat16)
        g_slots = jnp.take(pre_grad, up_col, axis=1).astype(jnp.float32)
        up_terms = group_sum(x_slots, g_slots, up_live)
        return total + partial_value, (up_terms, down_terms)

    total, grads = lax.scan(one_shard, jnp.zeros((TOKENS, D), jnp.float32), pieces)
    up_grads, down_grads = grads
    return (total.astype(jnp.bfloat16), up_grads.reshape(SLOTS, BLK, BLK), down_grads.reshape(SLOTS, BLK, BLK))
```

```python
import functools

import jax
import jax.numpy as jnp
from jax import lax
from jax.experimental import pallas as pl
from jax.experimental.pallas import tpu as pltpu
from jax.sharding import PartitionSpec as P

FF = 12288
GELU_C = 0.7978845608028654
VMEM_BYTES = 52 * 1024 * 1024


def bent_tanh(value):
    return jnp.tanh(GELU_C * (value + 0.044715 * value * value * value))


def gelu_slope(value, bent):
    return 0.5 * (1.0 + bent) + 0.5 * value * (1.0 - bent * bent) * GELU_C * (
        1.0 + 3.0 * 0.044715 * value * value
    )


def slot_rows(slices):
    ring, both, columns = slices.shape
    wide = slices.astype(jnp.float32)
    half = both // 2
    first = wide[:, :half].reshape(ring * half, columns)
    second = wide[:, half:].reshape(ring * half, columns)
    return jnp.concatenate([first, second], axis=0).astype(jnp.bfloat16)


def ring_rows(block, ring, both):
    half = both // 2
    rows, columns = block.shape
    first = block[: rows // 2].reshape(ring, half, columns)
    second = block[rows // 2 :].reshape(ring, half, columns)
    return jnp.concatenate([first, second], axis=1).astype(jnp.bfloat16)


def span(number, block):
    return pl.ds(pl.multiple_of(number * block, block), block)


def place_up(index, count, slots, dense, per_row):
    block = slots.shape[-1]
    dense[...] = jnp.zeros_like(dense)

    def place(s, _):
        row, column = lax.div(index[s], per_row), lax.rem(index[s], per_row)
        dense[span(row, block), span(column, block)] = slot_rows(slots[:, s])
        return 0

    lax.fori_loop(0, count[0], place, 0)


def place_down(index, count, slots, first, dense, per_row):
    block = slots.shape[-1]
    dense[...] = jnp.zeros_like(dense)

    def place(s, _):
        row, column = lax.div(index[s], per_row), lax.rem(index[s], per_row)
        dense[span(column, block), span(row, block)] = slot_rows(slots[:, first + s])
        return 0

    lax.fori_loop(0, count[0], place, 0)


def terms_kernel(
    up_index, up_count, down_index, down_count, x, x_t, dy, slots, terms, hidden, up, down, grad, hidden_t
):
    ring, both_slots, both, block = slots.shape
    cap = both_slots // 2
    per_row = up.shape[1] // block
    place_up(up_index, up_count, slots, up, per_row)
    place_down(down_index, down_count, slots, cap, down, per_row)
    for column in range(per_row):
        part = slice(column * block, (column + 1) * block)
        pre = jnp.dot(x[...], up[:, part], preferred_element_type=jnp.float32)
        bent = bent_tanh(pre)
        unit = 0.5 * pre * (1.0 + bent)
        hidden[:, part] = unit.astype(jnp.bfloat16)
        hidden_t[part, :] = jnp.transpose(unit).astype(jnp.bfloat16)
        back = lax.dot_general(
            dy[...], down[part, :], (((1,), (1,)), ((), ())), preferred_element_type=jnp.float32
        )
        grad[column] = (back * gelu_slope(pre, bent)).astype(jnp.bfloat16)

    def term(s, _):
        row, column = lax.div(down_index[s], per_row), lax.rem(down_index[s], per_row)
        live = (s < down_count[0]).astype(jnp.float32)
        value = jnp.dot(
            hidden_t[span(column, block), :], dy[:, span(row, block)], preferred_element_type=jnp.float32
        )
        terms[:, cap + s] = ring_rows(value * live, ring, both)
        row, column = lax.div(up_index[s], per_row), lax.rem(up_index[s], per_row)
        live = (s < up_count[0]).astype(jnp.float32)
        value = jnp.dot(x_t[span(row, block), :], grad[column], preferred_element_type=jnp.float32)
        terms[:, s] = ring_rows(value * live, ring, both)
        return 0

    lax.fori_loop(0, cap, term, 0, unroll=2)


def partial_kernel(down_index, down_count, hidden, slots, out, down):
    cap, block = slots.shape[1] // 2, slots.shape[3]
    per_row = hidden.shape[1] // block
    place_down(down_index, down_count, slots, cap, down, per_row)
    step = 2 * block
    for at in range(0, out.shape[1], step):
        out[:, at : at + step] = jnp.dot(
            hidden[...], down[:, at : at + step], preferred_element_type=jnp.float32
        ).astype(jnp.bfloat16)


SCALARS = pl.BlockSpec(memory_space=pltpu.SMEM)
WHOLE = pl.BlockSpec(memory_space=pltpu.VMEM)


def all_terms(up_index, up_count, down_index, down_count, x, x_t, dy, slots, units):
    rows, width = x.shape
    block = slots.shape[3]
    flops = 2 * rows * width * units * 2 + 2 * rows * block * block * slots.shape[1]
    return pl.pallas_call(
        terms_kernel,
        out_shape=(
            jax.ShapeDtypeStruct(slots.shape, jnp.bfloat16),
            jax.ShapeDtypeStruct((rows, units), jnp.bfloat16),
        ),
        in_specs=[SCALARS] * 4 + [WHOLE] * 4,
        out_specs=(WHOLE, WHOLE),
        scratch_shapes=[
            pltpu.VMEM((width, units), jnp.bfloat16),
            pltpu.VMEM((units, width), jnp.bfloat16),
            pltpu.VMEM((units // block, rows, block), jnp.bfloat16),
            pltpu.VMEM((units, rows), jnp.bfloat16),
        ],
        compiler_params=pltpu.CompilerParams(vmem_limit_bytes=VMEM_BYTES),
        cost_estimate=pl.CostEstimate(flops=flops, bytes_accessed=4 * slots.size, transcendentals=rows * units),
        name="terms",
    )(up_index, up_count, down_index, down_count, x, x_t, dy, slots)


def partial_sum(down_index, down_count, hidden, slots, width):
    rows, units = hidden.shape
    return pl.pallas_call(
        partial_kernel,
        out_shape=jax.ShapeDtypeStruct((rows, width), jnp.bfloat16),
        in_specs=[SCALARS] * 2 + [WHOLE] * 2,
        out_specs=WHOLE,
        scratch_shapes=[pltpu.VMEM((units, width), jnp.bfloat16)],
        compiler_params=pltpu.CompilerParams(vmem_limit_bytes=VMEM_BYTES),
        cost_estimate=pl.CostEstimate(
            flops=2 * rows * units * width, bytes_accessed=2 * slots.size, transcendentals=0
        ),
        name="partial",
    )(down_index, down_count, hidden, slots)


def spread(value, shards):
    copies = jnp.broadcast_to(value[None], (shards,) + value.shape)
    got = lax.all_to_all(copies, "tensor", split_axis=0, concat_axis=0, tiled=True)
    return got.reshape((shards * value.shape[0],) + value.shape[1:])


def body(tokens, cotangent, up_blocks, down_blocks, up_index, up_count, down_index, down_count):
    cap, part, block = up_blocks.shape
    groups = lax.axis_size("dp")
    shards = lax.axis_size("tensor")
    ring = groups // 2
    rings = [list(range(ring)), list(range(ring, groups))]
    across = [(i, (i + ring) % groups) for i in range(groups)]
    upper = lax.axis_index("dp") >= ring
    own = jnp.concatenate([up_blocks, down_blocks], axis=0)
    other = lax.ppermute(own, "dp", across)
    pair = jnp.concatenate(
        [jnp.where(upper, other, own), jnp.where(upper, own, other)], axis=1
    )
    slots = lax.all_gather(
        pair.reshape(2 * cap * 2 * part, block), "dp", axis=0, tiled=True, axis_index_groups=rings
    ).reshape(ring, 2 * cap, 2 * part, block)
    x = spread(tokens, shards)
    dy = spread(cotangent, shards)
    rows, width = x.shape
    terms, hidden = all_terms(
        up_index, up_count, down_index, down_count, x, x.T, dy, slots, FF // shards
    )
    summed = lax.psum_scatter(
        terms.reshape(ring * 2 * cap * 2 * part, block),
        "dp",
        scatter_dimension=0,
        tiled=True,
        axis_index_groups=rings,
    ).reshape(2 * cap, 2 * part, block)
    value = partial_sum(down_index, down_count, hidden, slots, width)
    got = lax.all_to_all(
        value.reshape(shards, rows // shards, width), "tensor", split_axis=0, concat_axis=0, tiled=True
    )
    mixed = jnp.sum(got.astype(jnp.float32), axis=0).astype(jnp.bfloat16)
    low, high = summed[:, :part], summed[:, part:]
    far = lax.ppermute(jnp.where(upper, low, high), "dp", across)
    grads = jnp.where(upper, high, low).astype(jnp.float32) + far.astype(jnp.float32)
    return (mixed, grads[:cap], grads[cap:])


def solution(mesh):
    in_specs = (
        P(("dp", "tensor"), None),
        P(("dp", "tensor"), None),
        P("tensor", "dp", None),
        P("tensor", "dp", None),
        P("tensor"),
        P("tensor"),
        P("tensor"),
        P("tensor"),
    )
    out_specs = (P(("dp", "tensor"), None), P("tensor", "dp", None), P("tensor", "dp", None))
    return jax.shard_map(body, mesh=mesh, in_specs=in_specs, out_specs=out_specs, check_vma=False)
```

```python
import functools

import jax
import jax.numpy as jnp
from jax import lax
from jax.experimental import pallas as pl
from jax.experimental.pallas import tpu as pltpu
from jax.sharding import PartitionSpec as P

FF = 12288
GELU_C = 0.7978845608028654
VMEM_BYTES = 34 * 1024 * 1024
CHUNKS = 4


def bent_tanh(value):
    return jnp.tanh(GELU_C * (value + 0.044715 * value * value * value))


def gelu_slope(value, bent):
    return 0.5 * (1.0 + bent) + 0.5 * value * (1.0 - bent * bent) * GELU_C * (
        1.0 + 3.0 * 0.044715 * value * value
    )


def own_rows(wide, ring, kind):
    part = wide.shape[1] // 4
    columns = wide.shape[2]
    pieces = [
        wide[:, (2 * pair + kind) * part : (2 * pair + kind + 1) * part].reshape(ring * part, columns)
        for pair in range(2)
    ]
    return jnp.concatenate(pieces, axis=0).astype(jnp.bfloat16)


def sent_rows(up, down, ring):
    rows, columns = up.shape
    part = rows // (2 * ring)
    pieces = [
        block[pair * rows // 2 : (pair + 1) * rows // 2].reshape(ring, part, columns)
        for pair in range(2)
        for block in (up, down)
    ]
    return jnp.concatenate(pieces, axis=1).astype(jnp.bfloat16)


def span(number, block):
    return pl.ds(pl.multiple_of(number * block, block), block)


def place_down(index, count, slots, s, dense, per_row):
    ring, block = slots.shape[0], slots.shape[-1]

    @pl.when(s < count[0])
    def _():
        row, column = lax.div(index[s], per_row), lax.rem(index[s], per_row)
        wide = slots[:, s].astype(jnp.float32)
        dense[span(column, block), span(row, block)] = own_rows(wide, ring, 1)


def place_up(index, count, slots, s, dense, per_row):
    ring, block = slots.shape[0], slots.shape[-1]

    @pl.when(s < count[0])
    def _():
        row, column = lax.div(index[s], per_row), lax.rem(index[s], per_row)
        wide = slots[:, s].astype(jnp.float32)
        dense[span(row, block), span(column, block)] = own_rows(wide, ring, 0)


def terms_kernel(
    up_index, up_count, down_index, down_count, x_far, x_t_far, dy_far, slots, terms, hidden,
    held, x, x_t, dy, up, down, grad, hidden_t, arrived, left,
):
    ring, cap, both, block = slots.shape
    per_row = up.shape[1] // block
    chunk = cap // CHUNKS
    part_of = [pl.ds(i * chunk, chunk) for i in range(CHUNKS)]
    incoming = [
        pltpu.make_async_copy(slots.at[:, at], held.at[:, at], arrived.at[i]) for i, at in enumerate(part_of)
    ]
    outgoing = [
        pltpu.make_async_copy(held.at[:, at], terms.at[:, at], left.at[i]) for i, at in enumerate(part_of)
    ]
    operands = [
        pltpu.make_async_copy(far, near, arrived.at[CHUNKS + i])
        for i, (far, near) in enumerate(((x_far, x), (dy_far, dy), (x_t_far, x_t)))
    ]
    for copy in incoming + operands:
        copy.start()
    up[...] = jnp.zeros_like(up)
    down[...] = jnp.zeros_like(down)

    def place(s, _):
        place_up(up_index, up_count, held, s, up, per_row)
        place_down(down_index, down_count, held, s, down, per_row)
        return 0

    for i in range(CHUNKS):
        incoming[i].wait()
        lax.fori_loop(i * chunk, (i + 1) * chunk, place, 0)
    operands[0].wait()
    operands[1].wait()
    for column in range(per_row):
        part = slice(column * block, (column + 1) * block)
        pre = jnp.dot(x[...], up[:, part], preferred_element_type=jnp.float32)
        bent = bent_tanh(pre)
        unit = 0.5 * pre * (1.0 + bent)
        hidden[:, part] = unit.astype(jnp.bfloat16)
        hidden_t[part, :] = jnp.transpose(unit).astype(jnp.bfloat16)
        back = lax.dot_general(
            dy[...], down[part, :], (((1,), (1,)), ((), ())), preferred_element_type=jnp.float32
        )
        grad[column] = (back * gelu_slope(pre, bent)).astype(jnp.bfloat16)

    operands[2].wait()

    def term(s, _):
        row, column = lax.div(down_index[s], per_row), lax.rem(down_index[s], per_row)
        down_term = jnp.dot(
            hidden_t[span(column, block), :], dy[:, span(row, block)], preferred_element_type=jnp.float32
        ) * (s < down_count[0]).astype(jnp.float32)
        row, column = lax.div(up_index[s], per_row), lax.rem(up_index[s], per_row)
        up_term = jnp.dot(
            x_t[span(row, block), :], grad[column], preferred_element_type=jnp.float32
        ) * (s < up_count[0]).astype(jnp.float32)
        held[:, s] = sent_rows(up_term, down_term, ring)
        return 0

    for i in range(CHUNKS):
        lax.fori_loop(i * chunk, (i + 1) * chunk, term, 0, unroll=chunk)
        outgoing[i].start()
    for copy in outgoing:
        copy.wait()


def partial_kernel(down_index, down_count, hidden, slots, out, down):
    cap, block = slots.shape[1], slots.shape[3]
    per_row = hidden.shape[1] // block
    down[...] = jnp.zeros_like(down)

    def place(s, _):
        place_down(down_index, down_count, slots, s, down, per_row)
        return 0

    lax.fori_loop(0, cap, place, 0)
    step = 2 * block
    for at in range(0, out.shape[1], step):
        out[:, at : at + step] = jnp.dot(
            hidden[...], down[:, at : at + step], preferred_element_type=jnp.float32
        ).astype(jnp.bfloat16)


SCALARS = pl.BlockSpec(memory_space=pltpu.SMEM)
WHOLE = pl.BlockSpec(memory_space=pltpu.VMEM)
FAR = pl.BlockSpec(memory_space=pltpu.HBM)


def all_terms(up_index, up_count, down_index, down_count, x, x_t, dy, slots, units):
    rows, width = x.shape
    block = slots.shape[3]
    far = [pltpu.with_memory_space_constraint(value, pltpu.HBM) for value in (x, x_t, dy, slots)]
    flops = 2 * rows * width * units * 2 + 4 * rows * block * block * slots.shape[1]
    return pl.pallas_call(
        terms_kernel,
        out_shape=(
            pltpu.HBM(slots.shape, jnp.bfloat16),
            jax.ShapeDtypeStruct((rows, units), jnp.bfloat16),
        ),
        in_specs=[SCALARS] * 4 + [FAR] * 4,
        out_specs=(FAR, WHOLE),
        scratch_shapes=[
            pltpu.VMEM(slots.shape, jnp.bfloat16),
            pltpu.VMEM((rows, width), jnp.bfloat16),
            pltpu.VMEM((width, rows), jnp.bfloat16),
            pltpu.VMEM((rows, width), jnp.bfloat16),
            pltpu.VMEM((width, units), jnp.bfloat16),
            pltpu.VMEM((units, width), jnp.bfloat16),
            pltpu.VMEM((units // block, rows, block), jnp.bfloat16),
            pltpu.VMEM((units, rows), jnp.bfloat16),
            pltpu.SemaphoreType.DMA((CHUNKS + 3,)),
            pltpu.SemaphoreType.DMA((CHUNKS,)),
        ],
        compiler_params=pltpu.CompilerParams(vmem_limit_bytes=VMEM_BYTES),
        cost_estimate=pl.CostEstimate(flops=flops, bytes_accessed=4 * slots.size, transcendentals=rows * units),
        name="terms",
    )(up_index, up_count, down_index, down_count, *far)


def partial_sum(down_index, down_count, hidden, slots, width):
    rows, units = hidden.shape
    return pl.pallas_call(
        partial_kernel,
        out_shape=jax.ShapeDtypeStruct((rows, width), jnp.bfloat16),
        in_specs=[SCALARS] * 2 + [WHOLE] * 2,
        out_specs=WHOLE,
        scratch_shapes=[pltpu.VMEM((units, width), jnp.bfloat16)],
        compiler_params=pltpu.CompilerParams(vmem_limit_bytes=VMEM_BYTES),
        cost_estimate=pl.CostEstimate(
            flops=2 * rows * units * width, bytes_accessed=2 * slots.size, transcendentals=0
        ),
        name="partial",
    )(down_index, down_count, hidden, slots)


def spread(value, shards):
    copies = jnp.broadcast_to(value[None], (shards,) + value.shape)
    got = lax.all_to_all(copies, "tensor", split_axis=0, concat_axis=0, tiled=True)
    return got.reshape((shards * value.shape[0],) + value.shape[1:])


def side_by_side(first, left, right):
    both = jnp.where(first[None, :, None, None], left[:, None], right[:, None])
    return both.reshape(left.shape[0], 2 * left.shape[1], left.shape[2])


def body(tokens, cotangent, up_blocks, down_blocks, up_index, up_count, down_index, down_count):
    cap, part, block = up_blocks.shape
    groups = lax.axis_size("dp")
    shards = lax.axis_size("tensor")
    ring = groups // 2
    rings = [list(range(ring)), list(range(ring, groups))]
    across = [(i, (i + ring) % groups) for i in range(groups)]
    own = side_by_side(jnp.arange(2) == 0, up_blocks, down_blocks)
    other = lax.ppermute(own, "dp", across)
    upper = lax.axis_index("dp") >= ring
    pair = side_by_side((jnp.arange(2) == 1) == upper, own, other)
    slots = lax.all_gather(
        pair.reshape(cap * 4 * part, block), "dp", axis=0, tiled=True, axis_index_groups=rings
    ).reshape(ring, cap, 4 * part, block)
    x = spread(tokens, shards)
    dy = spread(cotangent, shards)
    rows, width = x.shape
    terms, hidden = all_terms(
        up_index, up_count, down_index, down_count, x, x.T, dy, slots, FF // shards
    )
    summed = lax.psum_scatter(
        terms.reshape(ring * cap * 4 * part, block),
        "dp",
        scatter_dimension=0,
        tiled=True,
        axis_index_groups=rings,
    ).reshape(cap, 4 * part, block)
    value = partial_sum(down_index, down_count, hidden, slots, width)
    got = lax.all_to_all(
        value.reshape(shards, rows // shards, width), "tensor", split_axis=0, concat_axis=0, tiled=True
    )
    mixed = jnp.sum(got.astype(jnp.float32), axis=0).astype(jnp.bfloat16)
    low, high = summed[:, : 2 * part], summed[:, 2 * part :]
    far = lax.ppermute(jnp.where(upper, low, high), "dp", across)
    grads = jnp.where(upper, high, low).astype(jnp.float32) + far.astype(jnp.float32)
    return (mixed, grads[:, :part], grads[:, part:])


def solution(mesh):
    in_specs = (
        P(("dp", "tensor"), None),
        P(("dp", "tensor"), None),
        P("tensor", "dp", None),
        P("tensor", "dp", None),
        P("tensor"),
        P("tensor"),
        P("tensor"),
        P("tensor"),
    )
    out_specs = (P(("dp", "tensor"), None), P("tensor", "dp", None), P("tensor", "dp", None))
    return jax.shard_map(body, mesh=mesh, in_specs=in_specs, out_specs=out_specs, check_vma=False)
```

```python
import jax
import jax.numpy as jnp
from jax import lax
from jax.experimental import pallas as pl
from jax.experimental.pallas import tpu as pltpu
from jax.sharding import Mesh
from jax.sharding import PartitionSpec as P

FF = 12288
GELU_C = 0.7978845608028654
VMEM_BYTES = 36 * 1024 * 1024
CHUNKS = 4
PAIR, RING, PLANE, CORE = "y_lo", "z", "yx", "core"
SCALARS = pl.BlockSpec(memory_space=pltpu.SMEM)
WHOLE = pl.BlockSpec(memory_space=pltpu.VMEM)
FAR = pl.BlockSpec(memory_space=pltpu.HBM)


def bent_tanh(value):
    return jnp.tanh(GELU_C * (value + 0.044715 * value * value * value))


def gelu_slope(value, bent):
    return 0.5 * (1.0 + bent) + 0.5 * value * (1.0 - bent * bent) * GELU_C * (
        1.0 + 3.0 * 0.044715 * value * value
    )


def quarter(wide, number):
    ring, rows, half = wide.shape
    part = rows // 4
    return wide[:, number * part : (number + 1) * part].reshape(ring * part, half)


def up_half(wide):
    return jnp.concatenate([quarter(wide, 0), quarter(wide, 1)], axis=0).astype(jnp.bfloat16)


def down_half(wide):
    return jnp.concatenate([quarter(wide, 2), quarter(wide, 3)], axis=1).astype(jnp.bfloat16)


def sent_rows(up, down, ring):
    half = up.shape[1]
    pieces = [up[:half], up[half:], down[:, :half], down[:, half:]]
    pieces = [piece.reshape(ring, half // ring, half) for piece in pieces]
    return jnp.concatenate(pieces, axis=1).astype(jnp.bfloat16)


def span(number, size):
    return pl.ds(pl.multiple_of(number * size, size), size)


def place_up(index, count, slots, s, dense, per_row):
    half = slots.shape[3]

    @pl.when(s < count[0])
    def _():
        row, column = lax.div(index[s], per_row), lax.rem(index[s], per_row)
        dense[span(row, 2 * half), span(column, half)] = up_half(slots[:, s].astype(jnp.float32))


def place_down(index, count, slots, s, dense, per_row):
    half = slots.shape[3]

    @pl.when(s < count[0])
    def _():
        row, column = lax.div(index[s], per_row), lax.rem(index[s], per_row)
        dense[span(column, half), span(row, 2 * half)] = down_half(slots[:, s].astype(jnp.float32))


def terms_kernel(
    up_index, up_count, down_index, down_count, core, mine, other, slots, terms, hidden,
    held, x, dy, x_t, up, down, grad, hidden_t, arrived, left,
):
    ring, cap, _, half = slots.shape
    per_row = up.shape[1] // half
    rows, width = x.shape
    chunk = cap // CHUNKS
    part_of = [pl.ds(i * chunk, chunk) for i in range(CHUNKS)]
    incoming = [
        pltpu.make_async_copy(slots.at[:, at], held.at[:, at], arrived.at[i]) for i, at in enumerate(part_of)
    ]
    outgoing = [
        pltpu.make_async_copy(held.at[:, at], terms.at[:, at], left.at[i]) for i, at in enumerate(part_of)
    ]
    straight = [
        pltpu.make_async_copy(mine, x, arrived.at[CHUNKS]),
        pltpu.make_async_copy(other, dy, arrived.at[CHUNKS + 1]),
    ]
    crossed = [
        pltpu.make_async_copy(other, x, arrived.at[CHUNKS]),
        pltpu.make_async_copy(mine, dy, arrived.at[CHUNKS + 1]),
    ]
    for copy in incoming:
        copy.start()

    @pl.when(core[0] == 0)
    def _():
        for copy in straight:
            copy.start()

    @pl.when(core[0] != 0)
    def _():
        for copy in crossed:
            copy.start()

    up[...] = jnp.zeros_like(up)
    down[...] = jnp.zeros_like(down)

    def place(s, _):
        place_up(up_index, up_count, held, s, up, per_row)
        place_down(down_index, down_count, held, s, down, per_row)
        return 0

    for i in range(CHUNKS):
        incoming[i].wait()
        lax.fori_loop(i * chunk, (i + 1) * chunk, place, 0)

    @pl.when(core[0] == 0)
    def _():
        for copy in straight:
            copy.wait()

    @pl.when(core[0] != 0)
    def _():
        for copy in crossed:
            copy.wait()

    for at in range(0, rows, rows // 2):
        part = slice(at, at + rows // 2)
        pre = jnp.dot(x[part, :], up[...], preferred_element_type=jnp.float32)
        bent = bent_tanh(pre)
        unit = 0.5 * pre * (1.0 + bent)
        hidden[part, :] = unit.astype(jnp.bfloat16)
        hidden_t[:, part] = jnp.transpose(unit).astype(jnp.bfloat16)
        back = lax.dot_general(
            dy[part, :], down[...], (((1,), (1,)), ((), ())), preferred_element_type=jnp.float32
        )
        grad[part, :] = (back * gelu_slope(pre, bent)).astype(jnp.bfloat16)
    for at in range(0, width, 2 * half):
        x_t[at : at + 2 * half, :] = jnp.transpose(x[:, at : at + 2 * half])

    def term(s, _):
        row, column = lax.div(down_index[s], per_row), lax.rem(down_index[s], per_row)
        down_term = jnp.dot(
            hidden_t[span(column, half), :], dy[:, span(row, 2 * half)], preferred_element_type=jnp.float32
        ) * (s < down_count[0]).astype(jnp.float32)
        row, column = lax.div(up_index[s], per_row), lax.rem(up_index[s], per_row)
        up_term = jnp.dot(
            x_t[span(row, 2 * half), :], grad[:, span(column, half)], preferred_element_type=jnp.float32
        ) * (s < up_count[0]).astype(jnp.float32)
        held[:, s] = sent_rows(up_term, down_term, ring)
        return 0

    for i in range(CHUNKS):
        lax.fori_loop(i * chunk, (i + 1) * chunk, term, 0, unroll=chunk)
        outgoing[i].start()
    for copy in outgoing:
        copy.wait()


def partial_kernel(down_index, down_count, hidden, slots, out, down):
    cap, half = slots.shape[1], slots.shape[3]
    per_row = hidden.shape[1] // half
    down[...] = jnp.zeros_like(down)

    def place(s, _):
        place_down(down_index, down_count, slots, s, down, per_row)
        return 0

    lax.fori_loop(0, cap, place, 0)
    step = 4 * half
    for at in range(0, out.shape[1], step):
        out[:, at : at + step] = jnp.dot(
            hidden[...], down[:, at : at + step], preferred_element_type=jnp.float32
        ).astype(jnp.bfloat16)


def all_terms(up_index, up_count, down_index, down_count, core, mine, other, slots, units):
    rows, width = mine.shape
    flops = 4 * rows * width * units + 2 * rows * slots.size
    mine, other, slots = (pltpu.with_memory_space_constraint(v, pltpu.HBM) for v in (mine, other, slots))
    return pl.pallas_call(
        terms_kernel,
        out_shape=(
            pltpu.HBM(slots.shape, jnp.bfloat16),
            jax.ShapeDtypeStruct((rows, units), jnp.bfloat16),
        ),
        in_specs=[SCALARS] * 5 + [FAR] * 3,
        out_specs=(FAR, WHOLE),
        scratch_shapes=[
            pltpu.VMEM(slots.shape, jnp.bfloat16),
            pltpu.VMEM((rows, width), jnp.bfloat16),
            pltpu.VMEM((rows, width), jnp.bfloat16),
            pltpu.VMEM((width, rows), jnp.bfloat16),
            pltpu.VMEM((width, units), jnp.bfloat16),
            pltpu.VMEM((units, width), jnp.bfloat16),
            pltpu.VMEM((rows, units), jnp.bfloat16),
            pltpu.VMEM((units, rows), jnp.bfloat16),
            pltpu.SemaphoreType.DMA((CHUNKS + 2,)),
            pltpu.SemaphoreType.DMA((CHUNKS,)),
        ],
        compiler_params=pltpu.CompilerParams(vmem_limit_bytes=VMEM_BYTES),
        cost_estimate=pl.CostEstimate(flops=flops, bytes_accessed=4 * slots.size, transcendentals=rows * units),
        name="terms",
    )(up_index, up_count, down_index, down_count, core, mine, other, slots)


def partial_sum(down_index, down_count, hidden, slots, width):
    rows, units = hidden.shape
    return pl.pallas_call(
        partial_kernel,
        out_shape=pltpu.HBM((rows, width), jnp.bfloat16),
        in_specs=[SCALARS] * 2 + [WHOLE] * 2,
        out_specs=WHOLE,
        scratch_shapes=[pltpu.VMEM((units, width), jnp.bfloat16)],
        compiler_params=pltpu.CompilerParams(vmem_limit_bytes=VMEM_BYTES),
        cost_estimate=pl.CostEstimate(
            flops=2 * rows * units * width, bytes_accessed=2 * slots.size, transcendentals=0
        ),
        name="partial",
    )(down_index, down_count, hidden, slots)


def swapped(value, axis):
    return lax.ppermute(value, axis, [(0, 1), (1, 0)])


def body(tokens, cotangent, up_blocks, down_blocks, up_index, up_count, down_index, down_count):
    cap, part, block = up_blocks.shape
    ring = lax.axis_size(RING)
    shards = lax.axis_size(PLANE) * lax.axis_size(CORE)
    half = block // 2
    second = lax.axis_index(PAIR) == 1
    core = lax.axis_index(CORE)
    left, right = up_blocks[:, :, :half], up_blocks[:, :, half:]
    far = swapped(jnp.where(second, left, right), PAIR)
    near = jnp.where(second, right, left)
    rows, width = tokens.shape
    members = 2 * shards
    both = jnp.broadcast_to(jnp.stack([tokens, cotangent])[None], (shards, 2, rows, width))
    number = jnp.arange(4)[None, :, None, None]
    quarters = jnp.where(
        number < 2,
        jnp.where((number == 1) == second, near[:, None], far[:, None]),
        jnp.where(number == 2, down_blocks[:, None, :, :half], down_blocks[:, None, :, half:]),
    )
    slots = lax.all_gather(quarters.reshape(cap * 4 * part, half), RING, axis=0, tiled=True)
    slots = slots.reshape(ring, cap, 4 * part, half)
    mine = lax.cond(
        up_count[0] > 0,
        lambda value: lax.all_to_all(value, (PAIR, PLANE, CORE), split_axis=0, concat_axis=0, tiled=True),
        lambda value: value,
        both.reshape(members, rows, width),
    ).reshape(members * rows, width)
    other = swapped(mine, CORE)
    terms, hidden = all_terms(
        up_index, up_count, down_index, down_count, core.reshape(1), mine, other, slots, FF // members
    )
    summed = lax.psum_scatter(
        terms.reshape(ring * cap * 4 * part, half), RING, scatter_dimension=0, tiled=True
    ).reshape(cap, 4 * part, half)
    value = partial_sum(down_index, down_count, hidden, slots, width).reshape(members, rows, width)
    got = lax.all_to_all(value, (PAIR, PLANE, CORE), split_axis=0, concat_axis=0, tiled=True)
    mixed = jnp.sum(got.astype(jnp.float32), axis=0).astype(jnp.bfloat16)
    low, high = summed[:, :part], summed[:, part : 2 * part]
    far = swapped(jnp.where(second, low, high), PAIR)
    near = jnp.where(second, high, low)
    up_grad = jnp.concatenate([jnp.where(second, far, near), jnp.where(second, near, far)], axis=2)
    down_grad = jnp.concatenate([summed[:, 2 * part : 3 * part], summed[:, 3 * part :]], axis=2)
    return (mixed, up_grad.astype(jnp.float32), down_grad.astype(jnp.float32))


def solution(mesh):
    shape = mesh.devices.shape
    split = Mesh(mesh.devices.reshape(2, shape[0] // 2, shape[1] // 2, 2), (PAIR, RING, PLANE, CORE))
    by_rows = P((PAIR, RING, PLANE, CORE), None)
    by_blocks = P((PLANE, CORE), (PAIR, RING), None)
    by_shard = P((PLANE, CORE))
    return jax.shard_map(
        body,
        mesh=split,
        in_specs=(by_rows, by_rows, by_blocks, by_blocks, by_shard, by_shard, by_shard, by_shard),
        out_specs=(by_rows, by_blocks, by_blocks),
        check_vma=False,
    )
```

```python
import jax
import jax.numpy as jnp
from jax import lax
from jax.experimental import pallas as pl
from jax.experimental.pallas import tpu as pltpu
from jax.sharding import Mesh
from jax.sharding import PartitionSpec as P

FF = 12288
GELU_C = 0.7978845608028654
VMEM_BYTES = 36 * 1024 * 1024
CHUNKS = 4
STEPS = 2
PAIR, RING, PLANE, CORE = "y_lo", "z", "yx", "core"
SCALARS = pl.BlockSpec(memory_space=pltpu.SMEM)
WHOLE = pl.BlockSpec(memory_space=pltpu.VMEM)
FAR = pl.BlockSpec(memory_space=pltpu.HBM)


def bent_tanh(value):
    return jnp.tanh(GELU_C * (value + 0.044715 * value * value * value))


def gelu_slope(value, bent):
    return 0.5 * (1.0 + bent) + 0.5 * value * (1.0 - bent * bent) * GELU_C * (
        1.0 + 3.0 * 0.044715 * value * value
    )


def quarter(wide, number):
    ring, rows, half = wide.shape
    part = rows // 4
    return wide[:, number * part : (number + 1) * part].reshape(ring * part, half)


def up_half(wide):
    return jnp.concatenate([quarter(wide, 0), quarter(wide, 1)], axis=0).astype(jnp.bfloat16)


def down_half(wide):
    return jnp.concatenate([quarter(wide, 2), quarter(wide, 3)], axis=1).astype(jnp.bfloat16)


def sent_rows(up, down, ring):
    half = up.shape[1]
    pieces = [up[:half], up[half:], down[:, :half], down[:, half:]]
    pieces = [piece.reshape(ring, half // ring, half) for piece in pieces]
    return jnp.concatenate(pieces, axis=1).astype(jnp.bfloat16)


def span(number, size):
    return pl.ds(pl.multiple_of(number * size, size), size)


def place_up(index, count, slots, s, dense, per_row):
    half = slots.shape[3]

    @pl.when(s < count[0])
    def _():
        row, column = lax.div(index[s], per_row), lax.rem(index[s], per_row)
        dense[span(row, 2 * half), span(column, half)] = up_half(slots[:, s].astype(jnp.float32))


def place_down(index, count, slots, s, dense, per_row):
    half = slots.shape[3]

    @pl.when(s < count[0])
    def _():
        row, column = lax.div(index[s], per_row), lax.rem(index[s], per_row)
        dense[span(column, half), span(row, 2 * half)] = down_half(slots[:, s].astype(jnp.float32))


def terms_kernel(
    up_index, up_count, down_index, down_count, core, mine, other, slots, terms, hidden,
    held, x, dy, x_t, up, down, grad, hidden_t, arrived, left,
):
    ring, cap, _, half = slots.shape
    per_row = up.shape[1] // half
    rows, width = x.shape
    chunk = cap // CHUNKS
    part_of = [pl.ds(i * chunk, chunk) for i in range(CHUNKS)]
    incoming = [
        pltpu.make_async_copy(slots.at[:, at], held.at[:, at], arrived.at[i]) for i, at in enumerate(part_of)
    ]
    outgoing = [
        pltpu.make_async_copy(held.at[:, at], terms.at[:, at], left.at[i]) for i, at in enumerate(part_of)
    ]
    steps = [pl.ds(i * rows // STEPS, rows // STEPS) for i in range(STEPS)]

    def operands(first, second, i):
        at = steps[i]
        return (
            pltpu.make_async_copy(first.at[at], x.at[at], arrived.at[CHUNKS + 2 * i]),
            pltpu.make_async_copy(second.at[at], dy.at[at], arrived.at[CHUNKS + 2 * i + 1]),
        )

    def on_operands(act, i):
        @pl.when(core[0] == 0)
        def _():
            for copy in operands(mine, other, i):
                act(copy)

        @pl.when(core[0] != 0)
        def _():
            for copy in operands(other, mine, i):
                act(copy)

    for copy in incoming:
        copy.start()
    on_operands(lambda copy: copy.start(), 0)
    up[...] = jnp.zeros_like(up)
    down[...] = jnp.zeros_like(down)
    for i in range(1, STEPS):
        on_operands(lambda copy: copy.start(), i)

    def place(s, _):
        place_up(up_index, up_count, held, s, up, per_row)
        place_down(down_index, down_count, held, s, down, per_row)
        return 0

    for i in range(CHUNKS):
        incoming[i].wait()
        lax.fori_loop(i * chunk, (i + 1) * chunk, place, 0)

    for i, part in enumerate(steps):
        on_operands(lambda copy: copy.wait(), i)
        pre = jnp.dot(x[part, :], up[...], preferred_element_type=jnp.float32)
        bent = bent_tanh(pre)
        unit = 0.5 * pre * (1.0 + bent)
        hidden[part, :] = unit.astype(jnp.bfloat16)
        hidden_t[:, part] = jnp.transpose(unit).astype(jnp.bfloat16)
        back = lax.dot_general(
            dy[part, :], down[...], (((1,), (1,)), ((), ())), preferred_element_type=jnp.float32
        )
        grad[:, part] = jnp.transpose(back * gelu_slope(pre, bent)).astype(jnp.bfloat16)

    def term(s, _):
        row, column = lax.div(down_index[s], per_row), lax.rem(down_index[s], per_row)
        down_term = jnp.dot(
            hidden_t[span(column, half), :], dy[:, span(row, 2 * half)], preferred_element_type=jnp.float32
        ) * (s < down_count[0]).astype(jnp.float32)
        row, column = lax.div(up_index[s], per_row), lax.rem(up_index[s], per_row)
        up_term = jnp.transpose(jnp.dot(
            grad[span(column, half), :], x[:, span(row, 2 * half)], preferred_element_type=jnp.float32
        )) * (s < up_count[0]).astype(jnp.float32)
        held[:, s] = sent_rows(up_term, down_term, ring)
        return 0

    for i in range(CHUNKS):
        lax.fori_loop(i * chunk, (i + 1) * chunk, term, 0, unroll=chunk)
        outgoing[i].start()
    for copy in outgoing:
        copy.wait()


def partial_kernel(down_index, down_count, hidden, slots, out, down):
    cap, half = slots.shape[1], slots.shape[3]
    per_row = hidden.shape[1] // half
    down[...] = jnp.zeros_like(down)

    def place(s, _):
        place_down(down_index, down_count, slots, s, down, per_row)
        return 0

    lax.fori_loop(0, cap, place, 0)
    step = 4 * half
    for at in range(0, out.shape[1], step):
        out[:, at : at + step] = jnp.dot(
            hidden[...], down[:, at : at + step], preferred_element_type=jnp.float32
        ).astype(jnp.bfloat16)


def all_terms(up_index, up_count, down_index, down_count, core, mine, other, slots, units):
    rows, width = mine.shape
    flops = 4 * rows * width * units + 2 * rows * slots.size
    mine, other, slots = (pltpu.with_memory_space_constraint(v, pltpu.HBM) for v in (mine, other, slots))
    return pl.pallas_call(
        terms_kernel,
        out_shape=(
            pltpu.HBM(slots.shape, jnp.bfloat16),
            jax.ShapeDtypeStruct((rows, units), jnp.bfloat16),
        ),
        in_specs=[SCALARS] * 5 + [FAR] * 3,
        out_specs=(FAR, WHOLE),
        scratch_shapes=[
            pltpu.VMEM(slots.shape, jnp.bfloat16),
            pltpu.VMEM((rows, width), jnp.bfloat16),
            pltpu.VMEM((rows, width), jnp.bfloat16),
            pltpu.VMEM((width, rows), jnp.bfloat16),
            pltpu.VMEM((width, units), jnp.bfloat16),
            pltpu.VMEM((units, width), jnp.bfloat16),
            pltpu.VMEM((units, rows), jnp.bfloat16),
            pltpu.VMEM((units, rows), jnp.bfloat16),
            pltpu.SemaphoreType.DMA((CHUNKS + 2 * STEPS,)),
            pltpu.SemaphoreType.DMA((CHUNKS,)),
        ],
        compiler_params=pltpu.CompilerParams(vmem_limit_bytes=VMEM_BYTES),
        cost_estimate=pl.CostEstimate(flops=flops, bytes_accessed=4 * slots.size, transcendentals=rows * units),
        name="terms",
    )(up_index, up_count, down_index, down_count, core, mine, other, slots)


def partial_sum(down_index, down_count, hidden, slots, width):
    rows, units = hidden.shape
    return pl.pallas_call(
        partial_kernel,
        out_shape=pltpu.HBM((rows, width), jnp.bfloat16),
        in_specs=[SCALARS] * 2 + [WHOLE] * 2,
        out_specs=WHOLE,
        scratch_shapes=[pltpu.VMEM((units, width), jnp.bfloat16)],
        compiler_params=pltpu.CompilerParams(vmem_limit_bytes=VMEM_BYTES),
        cost_estimate=pl.CostEstimate(
            flops=2 * rows * units * width, bytes_accessed=2 * slots.size, transcendentals=0
        ),
        name="partial",
    )(down_index, down_count, hidden, slots)


def swapped(value, axis):
    return lax.ppermute(value, axis, [(0, 1), (1, 0)])


def body(tokens, cotangent, up_blocks, down_blocks, up_index, up_count, down_index, down_count):
    cap, part, block = up_blocks.shape
    ring = lax.axis_size(RING)
    shards = lax.axis_size(PLANE) * lax.axis_size(CORE)
    half = block // 2
    second = lax.axis_index(PAIR) == 1
    core = lax.axis_index(CORE)
    left, right = up_blocks[:, :, :half], up_blocks[:, :, half:]
    far = swapped(jnp.where(second, left, right), PAIR)
    near = jnp.where(second, right, left)
    rows, width = tokens.shape
    members = 2 * shards
    both = jnp.broadcast_to(jnp.stack([tokens, cotangent])[None], (shards, 2, rows, width))
    number = jnp.arange(4)[None, :, None, None]
    quarters = jnp.where(
        number < 2,
        jnp.where((number == 1) == second, near[:, None], far[:, None]),
        jnp.where(number == 2, down_blocks[:, None, :, :half], down_blocks[:, None, :, half:]),
    )
    slots = lax.all_gather(quarters.reshape(cap * 4 * part, half), RING, axis=0, tiled=True)
    slots = slots.reshape(ring, cap, 4 * part, half)
    mine = lax.cond(
        up_count[0] > 0,
        lambda value: lax.all_to_all(value, (PAIR, PLANE, CORE), split_axis=0, concat_axis=0, tiled=True),
        lambda value: value,
        both.reshape(members, rows, width),
    ).reshape(members * rows, width)
    other = swapped(mine, CORE)
    terms, hidden = all_terms(
        up_index, up_count, down_index, down_count, core.reshape(1), mine, other, slots, FF // members
    )
    summed = lax.psum_scatter(
        terms.reshape(ring * cap * 4 * part, half), RING, scatter_dimension=0, tiled=True
    ).reshape(cap, 4 * part, half)
    value = partial_sum(down_index, down_count, hidden, slots, width).reshape(shards, 2, rows, width)

    def over_plane(value):
        keep = lax.dynamic_index_in_dim(value, core, axis=1, keepdims=False)
        send = lax.dynamic_index_in_dim(value, 1 - core, axis=1, keepdims=False)
        added = (keep.astype(jnp.float32) + swapped(send, CORE).astype(jnp.float32)).astype(jnp.bfloat16)
        got = lax.all_to_all(added, (PAIR, PLANE), split_axis=0, concat_axis=0, tiled=True)
        return jnp.sum(got.astype(jnp.float32), axis=0).astype(jnp.bfloat16)

    mixed = lax.cond(up_count[0] > 0, over_plane, lambda value: value[0, 0], value)
    low, high = summed[:, :part], summed[:, part : 2 * part]
    far = swapped(jnp.where(second, low, high), PAIR)
    near = jnp.where(second, high, low)
    up_grad = jnp.concatenate([jnp.where(second, far, near), jnp.where(second, near, far)], axis=2)
    down_grad = jnp.concatenate([summed[:, 2 * part : 3 * part], summed[:, 3 * part :]], axis=2)
    return (mixed, up_grad.astype(jnp.float32), down_grad.astype(jnp.float32))


def solution(mesh):
    shape = mesh.devices.shape
    split = Mesh(mesh.devices.reshape(2, shape[0] // 2, shape[1] // 2, 2), (PAIR, RING, PLANE, CORE))
    by_rows = P((PAIR, RING, PLANE, CORE), None)
    by_blocks = P((PLANE, CORE), (PAIR, RING), None)
    by_shard = P((PLANE, CORE))
    return jax.shard_map(
        body,
        mesh=split,
        in_specs=(by_rows, by_rows, by_blocks, by_blocks, by_shard, by_shard, by_shard, by_shard),
        out_specs=(by_rows, by_blocks, by_blocks),
        check_vma=False,
    )
```

```python
import jax
import jax.numpy as jnp
from jax import lax
from jax.experimental import pallas as pl
from jax.experimental.pallas import tpu as pltpu
from jax.sharding import Mesh
from jax.sharding import PartitionSpec as P

FF = 12288
GELU_C = 0.7978845608028654
VMEM_BYTES = 36 * 1024 * 1024
CHUNKS = 4
STEPS = 2
PAIR, RING, PLANE, CORE = "y_lo", "z", "yx", "core"
SCALARS = pl.BlockSpec(memory_space=pltpu.SMEM)
WHOLE = pl.BlockSpec(memory_space=pltpu.VMEM)
FAR = pl.BlockSpec(memory_space=pltpu.HBM)


def bent_tanh(value):
    return jnp.tanh(GELU_C * (value + 0.044715 * value * value * value))


def gelu_slope(value, bent):
    return 0.5 * (1.0 + bent) + 0.5 * value * (1.0 - bent * bent) * GELU_C * (
        1.0 + 3.0 * 0.044715 * value * value
    )


def quarter(wide, number):
    ring, rows, half = wide.shape
    part = rows // 4
    return wide[:, number * part : (number + 1) * part].reshape(ring * part, half)


def up_half(wide):
    return jnp.concatenate([quarter(wide, 0), quarter(wide, 1)], axis=0).astype(jnp.bfloat16)


def down_half(wide):
    return jnp.concatenate([quarter(wide, 2), quarter(wide, 3)], axis=1).astype(jnp.bfloat16)


def sent_rows(up, down, ring):
    half = up.shape[1]
    pieces = [up[:half], up[half:], down[:, :half], down[:, half:]]
    pieces = [piece.reshape(ring, half // ring, half) for piece in pieces]
    return jnp.concatenate(pieces, axis=1).astype(jnp.bfloat16)


def span(number, size):
    return pl.ds(pl.multiple_of(number * size, size), size)


def place_up(index, count, slots, s, dense, per_row):
    half = slots.shape[3]

    @pl.when(s < count[0])
    def _():
        row, column = lax.div(index[s], per_row), lax.rem(index[s], per_row)
        dense[span(row, 2 * half), span(column, half)] = up_half(slots[:, s].astype(jnp.float32))


def place_down(index, count, slots, s, dense, per_row):
    half = slots.shape[3]

    @pl.when(s < count[0])
    def _():
        row, column = lax.div(index[s], per_row), lax.rem(index[s], per_row)
        dense[span(column, half), span(row, 2 * half)] = down_half(slots[:, s].astype(jnp.float32))


def terms_kernel(
    up_index, up_count, down_index, down_count, core, mine, other, slots, terms, hidden,
    held, x, dy, x_t, up, down, grad, hidden_t, arrived, left,
):
    ring, cap, _, half = slots.shape
    per_row = up.shape[1] // half
    rows, width = x.shape
    chunk = cap // CHUNKS
    part_of = [pl.ds(i * chunk, chunk) for i in range(CHUNKS)]
    incoming = [
        pltpu.make_async_copy(slots.at[:, at], held.at[:, at], arrived.at[i]) for i, at in enumerate(part_of)
    ]
    outgoing = [
        pltpu.make_async_copy(held.at[:, at], terms.at[:, at], left.at[i]) for i, at in enumerate(part_of)
    ]
    steps = [pl.ds(i * rows // STEPS, rows // STEPS) for i in range(STEPS)]

    def operands(first, second, i):
        at = steps[i]
        return (
            pltpu.make_async_copy(first.at[at], x.at[at], arrived.at[CHUNKS + 2 * i]),
            pltpu.make_async_copy(second.at[at], dy.at[at], arrived.at[CHUNKS + 2 * i + 1]),
        )

    def on_operands(act, i):
        @pl.when(core[0] == 0)
        def _():
            for copy in operands(mine, other, i):
                act(copy)

        @pl.when(core[0] != 0)
        def _():
            for copy in operands(other, mine, i):
                act(copy)

    for copy in incoming:
        copy.start()
    on_operands(lambda copy: copy.start(), 0)
    up[...] = jnp.zeros_like(up)
    down[...] = jnp.zeros_like(down)
    for i in range(1, STEPS):
        on_operands(lambda copy: copy.start(), i)

    def place(s, _):
        place_up(up_index, up_count, held, s, up, per_row)
        place_down(down_index, down_count, held, s, down, per_row)
        return 0

    for i in range(CHUNKS):
        incoming[i].wait()
        lax.fori_loop(i * chunk, (i + 1) * chunk, place, 0)

    for i, part in enumerate(steps):
        on_operands(lambda copy: copy.wait(), i)
        pre = jnp.dot(x[part, :], up[...], preferred_element_type=jnp.float32)
        bent = bent_tanh(pre)
        unit = 0.5 * pre * (1.0 + bent)
        hidden[part, :] = unit.astype(jnp.bfloat16)
        hidden_t[:, part] = jnp.transpose(unit).astype(jnp.bfloat16)
        back = lax.dot_general(
            dy[part, :], down[...], (((1,), (1,)), ((), ())), preferred_element_type=jnp.float32
        )
        grad[:, part] = jnp.transpose(back * gelu_slope(pre, bent)).astype(jnp.bfloat16)

    def term(s, _):
        row, column = lax.div(down_index[s], per_row), lax.rem(down_index[s], per_row)
        down_term = jnp.dot(
            hidden_t[span(column, half), :], dy[:, span(row, 2 * half)], preferred_element_type=jnp.float32
        ) * (s < down_count[0]).astype(jnp.float32)
        row, column = lax.div(up_index[s], per_row), lax.rem(up_index[s], per_row)
        up_term = jnp.transpose(jnp.dot(
            grad[span(column, half), :], x[:, span(row, 2 * half)], preferred_element_type=jnp.float32
        )) * (s < up_count[0]).astype(jnp.float32)
        held[:, s] = sent_rows(up_term, down_term, ring)
        return 0

    for i in range(CHUNKS):
        lax.fori_loop(i * chunk, (i + 1) * chunk, term, 0, unroll=chunk)
        outgoing[i].start()
    for copy in outgoing:
        copy.wait()


def partial_kernel(down_index, down_count, hidden, slots, out, down):
    cap, half = slots.shape[1], slots.shape[3]
    per_row = hidden.shape[1] // half
    down[...] = jnp.zeros_like(down)

    def place(s, _):
        place_down(down_index, down_count, slots, s, down, per_row)
        return 0

    lax.fori_loop(0, cap, place, 0)
    step = 4 * half
    for at in range(0, out.shape[1], step):
        out[:, at : at + step] = jnp.dot(
            hidden[...], down[:, at : at + step], preferred_element_type=jnp.float32
        ).astype(jnp.bfloat16)


def all_terms(up_index, up_count, down_index, down_count, core, mine, other, slots, units):
    rows, width = mine.shape
    flops = 4 * rows * width * units + 2 * rows * slots.size
    mine, other, slots = (pltpu.with_memory_space_constraint(v, pltpu.HBM) for v in (mine, other, slots))
    return pl.pallas_call(
        terms_kernel,
        out_shape=(
            pltpu.HBM(slots.shape, jnp.bfloat16),
            jax.ShapeDtypeStruct((rows, units), jnp.bfloat16),
        ),
        in_specs=[SCALARS] * 5 + [FAR] * 3,
        out_specs=(FAR, WHOLE),
        scratch_shapes=[
            pltpu.VMEM(slots.shape, jnp.bfloat16),
            pltpu.VMEM((rows, width), jnp.bfloat16),
            pltpu.VMEM((rows, width), jnp.bfloat16),
            pltpu.VMEM((width, rows), jnp.bfloat16),
            pltpu.VMEM((width, units), jnp.bfloat16),
            pltpu.VMEM((units, width), jnp.bfloat16),
            pltpu.VMEM((units, rows), jnp.bfloat16),
            pltpu.VMEM((units, rows), jnp.bfloat16),
            pltpu.SemaphoreType.DMA((CHUNKS + 2 * STEPS,)),
            pltpu.SemaphoreType.DMA((CHUNKS,)),
        ],
        compiler_params=pltpu.CompilerParams(vmem_limit_bytes=VMEM_BYTES),
        cost_estimate=pl.CostEstimate(flops=flops, bytes_accessed=4 * slots.size, transcendentals=rows * units),
        name="terms",
    )(up_index, up_count, down_index, down_count, core, mine, other, slots)


def partial_sum(down_index, down_count, hidden, slots, width):
    rows, units = hidden.shape
    return pl.pallas_call(
        partial_kernel,
        out_shape=pltpu.HBM((rows, width), jnp.bfloat16),
        in_specs=[SCALARS] * 2 + [WHOLE] * 2,
        out_specs=WHOLE,
        scratch_shapes=[pltpu.VMEM((units, width), jnp.bfloat16)],
        compiler_params=pltpu.CompilerParams(vmem_limit_bytes=VMEM_BYTES),
        cost_estimate=pl.CostEstimate(
            flops=2 * rows * units * width, bytes_accessed=2 * slots.size, transcendentals=0
        ),
        name="partial",
    )(down_index, down_count, hidden, slots)


def swapped(value, axis):
    return lax.ppermute(value, axis, [(0, 1), (1, 0)])


def body(tokens, cotangent, up_blocks, down_blocks, up_index, up_count, down_index, down_count):
    cap, part, block = up_blocks.shape
    ring = lax.axis_size(RING)
    shards = lax.axis_size(PLANE) * lax.axis_size(CORE)
    half = block // 2
    second = lax.axis_index(PAIR) == 1
    core = lax.axis_index(CORE)
    left, right = up_blocks[:, :, :half], up_blocks[:, :, half:]
    far = swapped(jnp.where(second, left, right), PAIR)
    near = jnp.where(second, right, left)
    packed, far = lax.optimization_barrier((jnp.stack([tokens, cotangent]), far))
    number = jnp.arange(4)[None, :, None, None]
    quarters = jnp.where(
        number < 2,
        jnp.where((number == 1) == second, near[:, None], far[:, None]),
        jnp.where(number == 2, down_blocks[:, None, :, :half], down_blocks[:, None, :, half:]),
    )
    slots = lax.all_gather(quarters.reshape(cap * 4 * part, half), RING, axis=0, tiled=True)
    slots = slots.reshape(ring, cap, 4 * part, half)
    rows, width = tokens.shape
    members = 2 * shards

    def copies(value):
        return jnp.broadcast_to(value[None], (shards,) + value.shape).reshape(members, rows, width)

    def spread(value):
        return lax.all_to_all(copies(value), (PAIR, PLANE, CORE), split_axis=0, concat_axis=0, tiled=True)

    always = core < 2
    mine = lax.cond(always, spread, copies, packed).reshape(members * rows, width)
    other = swapped(mine, CORE)
    terms, hidden = all_terms(
        up_index, up_count, down_index, down_count, core.reshape(1), mine, other, slots, FF // members
    )
    summed = lax.psum_scatter(
        terms.reshape(ring * cap * 4 * part, half), RING, scatter_dimension=0, tiled=True
    ).reshape(cap, 4 * part, half)
    value = partial_sum(down_index, down_count, hidden, slots, width).reshape(shards, 2, rows, width)

    def over_plane(value):
        keep = lax.dynamic_index_in_dim(value, core, axis=1, keepdims=False)
        send = lax.dynamic_index_in_dim(value, 1 - core, axis=1, keepdims=False)
        added = (keep.astype(jnp.float32) + swapped(send, CORE).astype(jnp.float32)).astype(jnp.bfloat16)
        got = lax.all_to_all(added, (PAIR, PLANE), split_axis=0, concat_axis=0, tiled=True)
        return jnp.sum(got.astype(jnp.float32), axis=0).astype(jnp.bfloat16)

    mixed = lax.cond(always, over_plane, lambda value: value[0, 0], value)
    low, high = summed[:, :part], summed[:, part : 2 * part]
    far = swapped(jnp.where(second, low, high), PAIR)
    up_grad = jnp.where(second, jnp.concatenate([far, high], axis=2), jnp.concatenate([low, far], axis=2))
    down_grad = jnp.concatenate([summed[:, 2 * part : 3 * part], summed[:, 3 * part :]], axis=2)
    return (mixed, up_grad.astype(jnp.float32), down_grad.astype(jnp.float32))


def solution(mesh):
    shape = mesh.devices.shape
    split = Mesh(mesh.devices.reshape(2, shape[0] // 2, shape[1] // 2, 2), (PAIR, RING, PLANE, CORE))
    by_rows = P((PAIR, RING, PLANE, CORE), None)
    by_blocks = P((PLANE, CORE), (PAIR, RING), None)
    by_shard = P((PLANE, CORE))
    return jax.shard_map(
        body,
        mesh=split,
        in_specs=(by_rows, by_rows, by_blocks, by_blocks, by_shard, by_shard, by_shard, by_shard),
        out_specs=(by_rows, by_blocks, by_blocks),
        check_vma=False,
    )
```

```python
import jax
import jax.numpy as jnp
from jax import lax
from jax.experimental import pallas as pl
from jax.experimental.pallas import tpu as pltpu
from jax.sharding import Mesh
from jax.sharding import PartitionSpec as P

FF = 12288
GELU_C = 0.7978845608028654
VMEM_BYTES = 36 * 1024 * 1024
CHUNKS = 4
STEPS = 2
PAIR, RING, PLANE, CORE = "y_lo", "z", "yx", "core"
SCALARS = pl.BlockSpec(memory_space=pltpu.SMEM)
WHOLE = pl.BlockSpec(memory_space=pltpu.VMEM)
FAR = pl.BlockSpec(memory_space=pltpu.HBM)


def bent_tanh(value):
    return jnp.tanh(GELU_C * (value + 0.044715 * value * value * value))


def gelu_slope(value, bent):
    return 0.5 * (1.0 + bent) + 0.5 * value * (1.0 - bent * bent) * GELU_C * (
        1.0 + 3.0 * 0.044715 * value * value
    )


def quarter(wide, number):
    ring, rows, half = wide.shape
    part = rows // 4
    return wide[:, number * part : (number + 1) * part].reshape(ring * part, half)


def up_half(wide):
    return jnp.concatenate([quarter(wide, 0), quarter(wide, 1)], axis=0).astype(jnp.bfloat16)


def down_half(wide):
    return jnp.concatenate([quarter(wide, 2), quarter(wide, 3)], axis=1).astype(jnp.bfloat16)


def sent_rows(up, down, ring):
    half = up.shape[1]
    pieces = [up[:half], up[half:], down[:, :half], down[:, half:]]
    pieces = [piece.reshape(ring, half // ring, half) for piece in pieces]
    return jnp.concatenate(pieces, axis=1).astype(jnp.bfloat16)


def span(number, size):
    return pl.ds(pl.multiple_of(number * size, size), size)


def place_up(index, count, slots, s, dense, per_row):
    half = slots.shape[3]

    @pl.when(s < count[0])
    def _():
        row, column = lax.div(index[s], per_row), lax.rem(index[s], per_row)
        dense[span(row, 2 * half), span(column, half)] = up_half(slots[:, s].astype(jnp.float32))


def place_down(index, count, slots, s, dense, per_row):
    half = slots.shape[3]

    @pl.when(s < count[0])
    def _():
        row, column = lax.div(index[s], per_row), lax.rem(index[s], per_row)
        dense[span(column, half), span(row, 2 * half)] = down_half(slots[:, s].astype(jnp.float32))


def terms_kernel(
    up_index, up_count, down_index, down_count, core, mine, other, slots, terms, hidden,
    held, x, dy, x_t, up, down, grad, hidden_t, arrived, left,
):
    ring, cap, _, half = slots.shape
    per_row = up.shape[1] // half
    rows, width = x.shape
    chunk = cap // CHUNKS
    part_of = [pl.ds(i * chunk, chunk) for i in range(CHUNKS)]
    incoming = [
        pltpu.make_async_copy(slots.at[:, at], held.at[:, at], arrived.at[i]) for i, at in enumerate(part_of)
    ]
    outgoing = [
        pltpu.make_async_copy(held.at[:, at], terms.at[:, at], left.at[i]) for i, at in enumerate(part_of)
    ]
    steps = [pl.ds(i * rows // STEPS, rows // STEPS) for i in range(STEPS)]

    def operands(first, second, i):
        at = steps[i]
        return (
            pltpu.make_async_copy(first.at[at], x.at[at], arrived.at[CHUNKS + 2 * i]),
            pltpu.make_async_copy(second.at[at], dy.at[at], arrived.at[CHUNKS + 2 * i + 1]),
        )

    def on_operands(act, i):
        @pl.when(core[0] == 0)
        def _():
            for copy in operands(mine, other, i):
                act(copy)

        @pl.when(core[0] != 0)
        def _():
            for copy in operands(other, mine, i):
                act(copy)

    for copy in incoming:
        copy.start()
    on_operands(lambda copy: copy.start(), 0)
    up[...] = jnp.zeros_like(up)
    down[...] = jnp.zeros_like(down)
    for i in range(1, STEPS):
        on_operands(lambda copy: copy.start(), i)

    def place(s, _):
        place_up(up_index, up_count, held, s, up, per_row)
        place_down(down_index, down_count, held, s, down, per_row)
        return 0

    for i in range(CHUNKS):
        incoming[i].wait()
        lax.fori_loop(i * chunk, (i + 1) * chunk, place, 0)

    for i, part in enumerate(steps):
        on_operands(lambda copy: copy.wait(), i)
        pre = jnp.dot(x[part, :], up[...], preferred_element_type=jnp.float32)
        bent = bent_tanh(pre)
        unit = 0.5 * pre * (1.0 + bent)
        hidden[part, :] = unit.astype(jnp.bfloat16)
        hidden_t[:, part] = jnp.transpose(unit).astype(jnp.bfloat16)
        back = lax.dot_general(
            dy[part, :], down[...], (((1,), (1,)), ((), ())), preferred_element_type=jnp.float32
        )
        grad[:, part] = jnp.transpose(back * gelu_slope(pre, bent)).astype(jnp.bfloat16)

    def term(s, _):
        row, column = lax.div(down_index[s], per_row), lax.rem(down_index[s], per_row)
        down_term = jnp.dot(
            hidden_t[span(column, half), :], dy[:, span(row, 2 * half)], preferred_element_type=jnp.float32
        ) * (s < down_count[0]).astype(jnp.float32)
        row, column = lax.div(up_index[s], per_row), lax.rem(up_index[s], per_row)
        up_term = jnp.transpose(jnp.dot(
            grad[span(column, half), :], x[:, span(row, 2 * half)], preferred_element_type=jnp.float32
        )) * (s < up_count[0]).astype(jnp.float32)
        held[:, s] = sent_rows(up_term, down_term, ring)
        return 0

    for i in range(CHUNKS):
        lax.fori_loop(i * chunk, (i + 1) * chunk, term, 0, unroll=chunk)
        outgoing[i].start()
    for copy in outgoing:
        copy.wait()


def partial_kernel(down_index, down_count, hidden, slots, out, down):
    cap, half = slots.shape[1], slots.shape[3]
    per_row = hidden.shape[1] // half
    down[...] = jnp.zeros_like(down)

    def place(s, _):
        place_down(down_index, down_count, slots, s, down, per_row)
        return 0

    lax.fori_loop(0, cap, place, 0)
    step = 4 * half
    for at in range(0, out.shape[1], step):
        out[:, at : at + step] = jnp.dot(
            hidden[...], down[:, at : at + step], preferred_element_type=jnp.float32
        ).astype(jnp.bfloat16)


def all_terms(up_index, up_count, down_index, down_count, core, mine, other, slots, units):
    rows, width = mine.shape
    flops = 4 * rows * width * units + 2 * rows * slots.size
    mine, other, slots = (pltpu.with_memory_space_constraint(v, pltpu.HBM) for v in (mine, other, slots))
    return pl.pallas_call(
        terms_kernel,
        out_shape=(
            pltpu.HBM(slots.shape, jnp.bfloat16),
            jax.ShapeDtypeStruct((rows, units), jnp.bfloat16),
        ),
        in_specs=[SCALARS] * 5 + [FAR] * 3,
        out_specs=(FAR, WHOLE),
        scratch_shapes=[
            pltpu.VMEM(slots.shape, jnp.bfloat16),
            pltpu.VMEM((rows, width), jnp.bfloat16),
            pltpu.VMEM((rows, width), jnp.bfloat16),
            pltpu.VMEM((width, rows), jnp.bfloat16),
            pltpu.VMEM((width, units), jnp.bfloat16),
            pltpu.VMEM((units, width), jnp.bfloat16),
            pltpu.VMEM((units, rows), jnp.bfloat16),
            pltpu.VMEM((units, rows), jnp.bfloat16),
            pltpu.SemaphoreType.DMA((CHUNKS + 2 * STEPS,)),
            pltpu.SemaphoreType.DMA((CHUNKS,)),
        ],
        compiler_params=pltpu.CompilerParams(vmem_limit_bytes=VMEM_BYTES),
        cost_estimate=pl.CostEstimate(flops=flops, bytes_accessed=4 * slots.size, transcendentals=rows * units),
        name="terms",
    )(up_index, up_count, down_index, down_count, core, mine, other, slots)


def partial_sum(down_index, down_count, hidden, slots, width):
    rows, units = hidden.shape
    return pl.pallas_call(
        partial_kernel,
        out_shape=pltpu.HBM((rows, width), jnp.bfloat16),
        in_specs=[SCALARS] * 2 + [WHOLE] * 2,
        out_specs=WHOLE,
        scratch_shapes=[pltpu.VMEM((units, width), jnp.bfloat16)],
        compiler_params=pltpu.CompilerParams(vmem_limit_bytes=VMEM_BYTES),
        cost_estimate=pl.CostEstimate(
            flops=2 * rows * units * width, bytes_accessed=2 * slots.size, transcendentals=0
        ),
        name="partial",
    )(down_index, down_count, hidden, slots)


def swapped(value, axis):
    return lax.ppermute(value, axis, [(0, 1), (1, 0)])


def body(tokens, cotangent, up_blocks, down_blocks, up_index, up_count, down_index, down_count):
    cap, part, block = up_blocks.shape
    ring = lax.axis_size(RING)
    shards = lax.axis_size(PLANE) * lax.axis_size(CORE)
    half = block // 2
    second = lax.axis_index(PAIR) == 1
    core = lax.axis_index(CORE)
    far = swapped(up_blocks, PAIR)
    packed, far = lax.optimization_barrier((jnp.stack([tokens, cotangent]), far))
    far = jnp.where(second, far[:, :, half:], far[:, :, :half])
    near = jnp.where(second, up_blocks[:, :, half:], up_blocks[:, :, :half])
    number = jnp.arange(4)[None, :, None, None]
    quarters = jnp.where(
        number < 2,
        jnp.where((number == 1) == second, near[:, None], far[:, None]),
        jnp.where(number == 2, down_blocks[:, None, :, :half], down_blocks[:, None, :, half:]),
    )
    slots = lax.all_gather(quarters.reshape(cap * 4 * part, half), RING, axis=0, tiled=True)
    slots = slots.reshape(ring, cap, 4 * part, half)
    rows, width = tokens.shape
    members = 2 * shards

    def copies(value):
        return jnp.broadcast_to(value[None], (shards,) + value.shape).reshape(members, rows, width)

    def spread(value):
        return lax.all_to_all(copies(value), (PAIR, PLANE, CORE), split_axis=0, concat_axis=0, tiled=True)

    always = core < 2
    mine = lax.cond(always, spread, copies, packed).reshape(members * rows, width)
    other = swapped(mine, CORE)
    terms, hidden = all_terms(
        up_index, up_count, down_index, down_count, core.reshape(1), mine, other, slots, FF // members
    )
    summed = lax.psum_scatter(
        terms.reshape(ring * cap * 4 * part, half), RING, scatter_dimension=0, tiled=True
    ).reshape(cap, 4 * part, half)
    value = partial_sum(down_index, down_count, hidden, slots, width).reshape(shards, 2, rows, width)

    def over_plane(value):
        keep = lax.dynamic_index_in_dim(value, core, axis=1, keepdims=False)
        send = lax.dynamic_index_in_dim(value, 1 - core, axis=1, keepdims=False)
        added = (keep.astype(jnp.float32) + swapped(send, CORE).astype(jnp.float32)).astype(jnp.bfloat16)
        got = lax.all_to_all(added, (PAIR, PLANE), split_axis=0, concat_axis=0, tiled=True)
        return jnp.sum(got.astype(jnp.float32), axis=0).astype(jnp.bfloat16)

    mixed = lax.cond(always, over_plane, lambda value: value[0, 0], value)
    low, high = summed[:, :part], summed[:, part : 2 * part]
    far = swapped(jnp.where(second, low, high), PAIR)
    up_grad = jnp.where(second, jnp.concatenate([far, high], axis=2), jnp.concatenate([low, far], axis=2))
    down_grad = jnp.concatenate([summed[:, 2 * part : 3 * part], summed[:, 3 * part :]], axis=2)
    return (mixed, up_grad.astype(jnp.float32), down_grad.astype(jnp.float32))


def solution(mesh):
    shape = mesh.devices.shape
    split = Mesh(mesh.devices.reshape(2, shape[0] // 2, shape[1] // 2, 2), (PAIR, RING, PLANE, CORE))
    by_rows = P((PAIR, RING, PLANE, CORE), None)
    by_blocks = P((PLANE, CORE), (PAIR, RING), None)
    by_shard = P((PLANE, CORE))
    return jax.shard_map(
        body,
        mesh=split,
        in_specs=(by_rows, by_rows, by_blocks, by_blocks, by_shard, by_shard, by_shard, by_shard),
        out_specs=(by_rows, by_blocks, by_blocks),
        check_vma=False,
    )
```

```python
import jax
import jax.numpy as jnp
from jax import lax
from jax.experimental import pallas as pl
from jax.experimental.pallas import tpu as pltpu
from jax.sharding import Mesh
from jax.sharding import PartitionSpec as P

FF = 12288
GELU_C = 0.7978845608028654
VMEM_BYTES = 36 * 1024 * 1024
CHUNKS = 4
STEPS = 2
PAIR, RING, PLANE, CORE = "y_lo", "z", "yx", "core"
SCALARS = pl.BlockSpec(memory_space=pltpu.SMEM)
WHOLE = pl.BlockSpec(memory_space=pltpu.VMEM)
FAR = pl.BlockSpec(memory_space=pltpu.HBM)


def bent_tanh(value):
    return jnp.tanh(GELU_C * (value + 0.044715 * value * value * value))


def gelu_slope(value, bent):
    return 0.5 * (1.0 + bent) + 0.5 * value * (1.0 - bent * bent) * GELU_C * (
        1.0 + 3.0 * 0.044715 * value * value
    )


def quarter(wide, number):
    ring, rows, half = wide.shape
    part = rows // 4
    return wide[:, number * part : (number + 1) * part].reshape(ring * part, half)


def up_half(wide):
    return jnp.concatenate([quarter(wide, 0), quarter(wide, 1)], axis=0).astype(jnp.bfloat16)


def down_half(wide):
    return jnp.concatenate([quarter(wide, 2), quarter(wide, 3)], axis=1).astype(jnp.bfloat16)


def sent_rows(up, down, ring):
    half = up.shape[1]
    pieces = [up[:half], up[half:], down[:, :half], down[:, half:]]
    pieces = [piece.reshape(ring, half // ring, half) for piece in pieces]
    return jnp.concatenate(pieces, axis=1).astype(jnp.bfloat16)


def span(number, size):
    return pl.ds(pl.multiple_of(number * size, size), size)


def place_up(index, count, slots, s, dense, per_row):
    half = slots.shape[3]

    @pl.when(s < count[0])
    def _():
        row, column = lax.div(index[s], per_row), lax.rem(index[s], per_row)
        dense[span(row, 2 * half), span(column, half)] = up_half(slots[:, s].astype(jnp.float32))


def place_down(index, count, slots, s, dense, per_row):
    half = slots.shape[3]

    @pl.when(s < count[0])
    def _():
        row, column = lax.div(index[s], per_row), lax.rem(index[s], per_row)
        dense[span(column, half), span(row, 2 * half)] = down_half(slots[:, s].astype(jnp.float32))


def terms_kernel(
    up_index, up_count, down_index, down_count, core, mine, other, slots, terms, hidden,
    held, x, dy, x_t, up, down, grad, hidden_t, arrived, left,
):
    ring, cap, _, half = slots.shape
    per_row = up.shape[1] // half
    rows, width = x.shape
    chunk = cap // CHUNKS
    part_of = [pl.ds(i * chunk, chunk) for i in range(CHUNKS)]
    incoming = [
        pltpu.make_async_copy(slots.at[:, at], held.at[:, at], arrived.at[i]) for i, at in enumerate(part_of)
    ]
    outgoing = [
        pltpu.make_async_copy(held.at[:, at], terms.at[:, at], left.at[i]) for i, at in enumerate(part_of)
    ]
    steps = [pl.ds(i * rows // STEPS, rows // STEPS) for i in range(STEPS)]

    def operands(first, second, i):
        at = steps[i]
        return (
            pltpu.make_async_copy(first.at[at], x.at[at], arrived.at[CHUNKS + 2 * i]),
            pltpu.make_async_copy(second.at[at], dy.at[at], arrived.at[CHUNKS + 2 * i + 1]),
        )

    def on_operands(act, i):
        @pl.when(core[0] == 0)
        def _():
            for copy in operands(mine, other, i):
                act(copy)

        @pl.when(core[0] != 0)
        def _():
            for copy in operands(other, mine, i):
                act(copy)

    for copy in incoming:
        copy.start()
    on_operands(lambda copy: copy.start(), 0)
    up[...] = jnp.zeros_like(up)
    down[...] = jnp.zeros_like(down)
    for i in range(1, STEPS):
        on_operands(lambda copy: copy.start(), i)

    def place(s, _):
        place_up(up_index, up_count, held, s, up, per_row)
        place_down(down_index, down_count, held, s, down, per_row)
        return 0

    for i in range(CHUNKS):
        incoming[i].wait()
        lax.fori_loop(i * chunk, (i + 1) * chunk, place, 0)

    for i, part in enumerate(steps):
        on_operands(lambda copy: copy.wait(), i)
        pre = jnp.dot(x[part, :], up[...], preferred_element_type=jnp.float32)
        bent = bent_tanh(pre)
        unit = 0.5 * pre * (1.0 + bent)
        hidden[part, :] = unit.astype(jnp.bfloat16)
        hidden_t[:, part] = jnp.transpose(unit).astype(jnp.bfloat16)
        back = lax.dot_general(
            dy[part, :], down[...], (((1,), (1,)), ((), ())), preferred_element_type=jnp.float32
        )
        grad[:, part] = jnp.transpose(back * gelu_slope(pre, bent)).astype(jnp.bfloat16)

    def term(s, _):
        row, column = lax.div(down_index[s], per_row), lax.rem(down_index[s], per_row)
        down_term = jnp.dot(
            hidden_t[span(column, half), :], dy[:, span(row, 2 * half)], preferred_element_type=jnp.float32
        ) * (s < down_count[0]).astype(jnp.float32)
        row, column = lax.div(up_index[s], per_row), lax.rem(up_index[s], per_row)
        up_term = jnp.transpose(jnp.dot(
            grad[span(column, half), :], x[:, span(row, 2 * half)], preferred_element_type=jnp.float32
        )) * (s < up_count[0]).astype(jnp.float32)
        held[:, s] = sent_rows(up_term, down_term, ring)
        return 0

    for i in range(CHUNKS):
        lax.fori_loop(i * chunk, (i + 1) * chunk, term, 0, unroll=chunk)
        outgoing[i].start()
    for copy in outgoing:
        copy.wait()


def partial_kernel(down_index, down_count, hidden, slots, out, down):
    cap, half = slots.shape[1], slots.shape[3]
    per_row = hidden.shape[1] // half
    down[...] = jnp.zeros_like(down)

    def place(s, _):
        place_down(down_index, down_count, slots, s, down, per_row)
        return 0

    lax.fori_loop(0, cap, place, 0)
    step = 4 * half
    for at in range(0, out.shape[1], step):
        out[:, at : at + step] = jnp.dot(
            hidden[...], down[:, at : at + step], preferred_element_type=jnp.float32
        ).astype(jnp.bfloat16)


def all_terms(up_index, up_count, down_index, down_count, core, mine, other, slots, units):
    rows, width = mine.shape
    flops = 4 * rows * width * units + 2 * rows * slots.size
    mine, other, slots = (pltpu.with_memory_space_constraint(v, pltpu.HBM) for v in (mine, other, slots))
    return pl.pallas_call(
        terms_kernel,
        out_shape=(
            pltpu.HBM(slots.shape, jnp.bfloat16),
            jax.ShapeDtypeStruct((rows, units), jnp.bfloat16),
        ),
        in_specs=[SCALARS] * 5 + [FAR] * 3,
        out_specs=(FAR, WHOLE),
        scratch_shapes=[
            pltpu.VMEM(slots.shape, jnp.bfloat16),
            pltpu.VMEM((rows, width), jnp.bfloat16),
            pltpu.VMEM((rows, width), jnp.bfloat16),
            pltpu.VMEM((width, rows), jnp.bfloat16),
            pltpu.VMEM((width, units), jnp.bfloat16),
            pltpu.VMEM((units, width), jnp.bfloat16),
            pltpu.VMEM((units, rows), jnp.bfloat16),
            pltpu.VMEM((units, rows), jnp.bfloat16),
            pltpu.SemaphoreType.DMA((CHUNKS + 2 * STEPS,)),
            pltpu.SemaphoreType.DMA((CHUNKS,)),
        ],
        compiler_params=pltpu.CompilerParams(vmem_limit_bytes=VMEM_BYTES),
        cost_estimate=pl.CostEstimate(flops=flops, bytes_accessed=4 * slots.size, transcendentals=rows * units),
        name="terms",
    )(up_index, up_count, down_index, down_count, core, mine, other, slots)


def partial_sum(down_index, down_count, hidden, slots, width):
    rows, units = hidden.shape
    return pl.pallas_call(
        partial_kernel,
        out_shape=pltpu.HBM((rows, width), jnp.bfloat16),
        in_specs=[SCALARS] * 2 + [WHOLE] * 2,
        out_specs=WHOLE,
        scratch_shapes=[pltpu.VMEM((units, width), jnp.bfloat16)],
        compiler_params=pltpu.CompilerParams(vmem_limit_bytes=VMEM_BYTES),
        cost_estimate=pl.CostEstimate(
            flops=2 * rows * units * width, bytes_accessed=2 * slots.size, transcendentals=0
        ),
        name="partial",
    )(down_index, down_count, hidden, slots)


def swapped(value, axis):
    return lax.ppermute(value, axis, [(0, 1), (1, 0)])


def body(tokens, cotangent, up_blocks, down_blocks, up_index, up_count, down_index, down_count):
    cap, part, block = up_blocks.shape
    ring = lax.axis_size(RING)
    shards = lax.axis_size(PLANE) * lax.axis_size(CORE)
    half = block // 2
    second = lax.axis_index(PAIR) == 1
    core = lax.axis_index(CORE)
    left, right = up_blocks[:, :, :half], up_blocks[:, :, half:]
    far = swapped(jnp.where(second, left, right), PAIR)
    near = jnp.where(second, right, left)
    number = jnp.arange(4)[None, :, None, None]
    laid = jnp.where(
        number < 2,
        near[:, None],
        jnp.where(number == 2, down_blocks[:, None, :, :half], down_blocks[:, None, :, half:]),
    )
    packed, laid, far = lax.optimization_barrier((jnp.stack([tokens, cotangent]), laid, far))
    quarters = jnp.where((number < 2) & ((number == 1) != second), far[:, None], laid)
    slots = lax.all_gather(quarters.reshape(cap * 4 * part, half), RING, axis=0, tiled=True)
    slots = slots.reshape(ring, cap, 4 * part, half)
    rows, width = tokens.shape
    members = 2 * shards

    def copies(value):
        return jnp.broadcast_to(value[None], (shards,) + value.shape).reshape(members, rows, width)

    def spread(value):
        return lax.all_to_all(copies(value), (PAIR, PLANE, CORE), split_axis=0, concat_axis=0, tiled=True)

    always = core < 2
    mine = lax.cond(always, spread, copies, packed).reshape(members * rows, width)
    other = swapped(mine, CORE)
    terms, hidden = all_terms(
        up_index, up_count, down_index, down_count, core.reshape(1), mine, other, slots, FF // members
    )
    summed = lax.psum_scatter(
        terms.reshape(ring * cap * 4 * part, half), RING, scatter_dimension=0, tiled=True
    ).reshape(cap, 4 * part, half)
    value = partial_sum(down_index, down_count, hidden, slots, width).reshape(shards, 2, rows, width)

    def over_plane(value):
        keep = lax.dynamic_index_in_dim(value, core, axis=1, keepdims=False)
        send = lax.dynamic_index_in_dim(value, 1 - core, axis=1, keepdims=False)
        added = (keep.astype(jnp.float32) + swapped(send, CORE).astype(jnp.float32)).astype(jnp.bfloat16)
        got = lax.all_to_all(added, (PAIR, PLANE), split_axis=0, concat_axis=0, tiled=True)
        return jnp.sum(got.astype(jnp.float32), axis=0).astype(jnp.bfloat16)

    mixed = lax.cond(always, over_plane, lambda value: value[0, 0], value)
    low, high = summed[:, :part], summed[:, part : 2 * part]
    far = swapped(jnp.where(second, low, high), PAIR)
    up_grad = jnp.where(second, jnp.concatenate([far, high], axis=2), jnp.concatenate([low, far], axis=2))
    down_grad = jnp.concatenate([summed[:, 2 * part : 3 * part], summed[:, 3 * part :]], axis=2)
    return (mixed, up_grad.astype(jnp.float32), down_grad.astype(jnp.float32))


def solution(mesh):
    shape = mesh.devices.shape
    split = Mesh(mesh.devices.reshape(2, shape[0] // 2, shape[1] // 2, 2), (PAIR, RING, PLANE, CORE))
    by_rows = P((PAIR, RING, PLANE, CORE), None)
    by_blocks = P((PLANE, CORE), (PAIR, RING), None)
    by_shard = P((PLANE, CORE))
    return jax.shard_map(
        body,
        mesh=split,
        in_specs=(by_rows, by_rows, by_blocks, by_blocks, by_shard, by_shard, by_shard, by_shard),
        out_specs=(by_rows, by_blocks, by_blocks),
        check_vma=False,
    )
```
